32 devices in a mesh: city: 2 (over y), blk: 4 (over z), band: 2 (over x), sub: 2 (over core).
Axes of the slice: x: 2, y: 2, z: 4, core: 2. Of those that a mesh axis runs over, the one named last changes fastest.
Arguments:
- positions: float32 [3, 8192], P(None, ('city', 'blk')), parts along dimension 1, may hold values from -1.25 to 1.25
- angles: float32 [2, 8192], P(None, ('city', 'blk')), parts along dimension 1, may hold values from -3.140625 to 3.140625
- area: float32 [1, 8192], P(None, ('city', 'blk')), parts along dimension 1, may hold values from 0.25 to 1
- vis_list: int32 [32, 8], P(('city', 'blk'), 'sub'), parts along dimension 0, may hold values from 0 to 15, as said below
- counts: int32 [32], P(('city', 'blk')), parts along dimension 0, may hold values from 1 to 8, as said below
- occl: int32 [32, 8, 16, 256], P(('city', 'blk'), 'sub'), parts along dimension 0, may hold values from 0 to 65535
- direct: float32 [16, 8192], P('band', ('city', 'blk')), parts along dimension 1, may hold values from 0.1 to 2
- reflect: float32 [16, 8192], P('band', ('city', 'blk')), parts along dimension 1, may hold values from 0.25 to 0.9
- band_frac: float32 [16], P('band'), may hold values from 0.02 to 0.2
- temp: float32 [8192], P(('city', 'blk')), parts along dimension 0, may hold values from 0.8 to 1.2
- heat: float32 [8192], P(('city', 'blk')), parts along dimension 0, may hold values from 0.02 to 0.2
Outputs:
- radiosity: float32 [16, 8192], P('band', ('city', 'blk')), parts along dimension 1
- new_temp: float32 [8192], P(('city', 'blk')), parts along dimension 0
The draws below stay inside these ranges and needn't reach their ends.
There are 2 independent parts, one for each index of `city`. The reference program is written for one: setup_inputs(seed, part) draws one part's arguments, and reference() takes and returns one part's arrays. A program takes and returns all parts, laid end to end along the dimension named above; an argument that names none is the same for every part. Nothing has to cross between parts.
Inputs may be any that keep to these rules, and one draw needn't show every extreme that they name: `vis_list`: row block r is held by index r // 4 of blk. Among the slots of the 4 row blocks of one index of blk that one index of sub holds, at most 4 name blocks held by any one index of blk, and for every such group of slots some index of blk holds exactly 4 of them. `counts`: some row block has all 8 slots valid.
All inputs are finite; a program needn't handle non-finite values.
Results may differ from the reference program's by a relative error of at most 0.0003.
Values sent between devices are 32-bit elements; how exact they have to be, the bound alone decides.
A program may use at most 128 MiB of HBM per device.

```python
import math
import jax
import jax.numpy as jnp
from jax import lax

BANDS = 16
BS = 256
LIST = 8
ITERS = 3
RB_DEV = 4
NROWB = 16
NF = 4096
CAP = 4
N_BLK = 4
N_SUB = 2


def draw_vis_list(key, part):
    key = jax.random.fold_in(key, 11)
    perm_key, base_key = jax.random.split(key)
    groups = N_BLK * N_SUB
    span = N_BLK * CAP
    width = RB_DEV * (LIST // N_SUB)
    scores = jax.random.randint(perm_key, (groups, span), 0, 2 ** 20) * span + jnp.arange(span, dtype=jnp.int32)[None, :]
    picked = jnp.argsort(scores, axis=1)[:, :width].astype(jnp.int32)
    holder = picked // CAP
    level = picked % CAP
    base_offset = jax.random.randint(base_key, (groups, N_BLK), 0, RB_DEV)
    start_offset = jnp.take_along_axis(base_offset, holder, axis=1)
    block_num = holder * RB_DEV + (start_offset + level) % RB_DEV
    block_num = block_num.reshape(N_BLK, N_SUB, RB_DEV, LIST // N_SUB)
    return jnp.transpose(block_num, (0, 2, 1, 3)).reshape(NROWB, LIST).astype(jnp.int32)


def draw_counts(key, part):
    key = jax.random.fold_in(key, 23)
    first_key, second_key = jax.random.split(key)
    drawn = jax.random.randint(first_key, (NROWB,), 1, LIST + 1)
    chosen = jax.random.randint(second_key, (), 0, NROWB)
    return jnp.where(jnp.arange(NROWB, dtype=jnp.int32) == chosen, LIST, drawn).astype(jnp.int32)


def set_ends(entries, stream_key, smallest, top_value):
    longest = entries.shape.index(max(entries.shape))
    spots = []
    for shift in (0, 1):
        where = [jax.random.randint(jax.random.fold_in(stream_key, axis), (), 0, length) for axis, length in enumerate(entries.shape)]
        where[longest] = (where[longest] + shift) % entries.shape[longest]
        spots.append(tuple(where))
    return entries.at[spots[0]].set(smallest).at[spots[1]].set(top_value)


def shard_levels(key, dims, cuts, smallest, largest):
    def one(dim, shards_of):
        heights = jax.random.uniform(jax.random.fold_in(jax.random.fold_in(key, 6), dim), (shards_of,), jnp.float32, smallest / len(cuts), largest / len(cuts))
        return jnp.repeat(jnp.exp(heights), dims[dim] // shards_of).reshape((-1,) + (1,) * (len(dims) - dim - 1))

    factor_of = one(*cuts[0])
    for cut in cuts[1:]:
        factor_of = factor_of * one(*cut)
    return factor_of


def setup_inputs(seed: int = 0, part: int = 0) -> dict:
    keys = jax.random.split(jax.random.key(seed), 12)
    part_keys = jax.random.split(jax.random.fold_in(keys[11], part), 12)
    positions = jnp.clip(jax.random.uniform(part_keys[0], (3, NF), jnp.float32, -1.25, 1.25) * shard_levels(part_keys[0], (3, NF), ((1, 4),), -0.4, 0.0), -1.25, 1.25)
    angles = jnp.clip(jax.random.uniform(part_keys[1], (2, NF), jnp.float32, -3.140625, 3.140625), -3.140625, 3.140625)
    area = jnp.clip(jnp.exp(math.log(1.0) - 1.3862944 * jax.random.uniform(part_keys[2], (1, NF), jnp.float32) ** shard_levels(part_keys[2], (1, NF), ((1, 4),), -0.2, 0.2)), 0.25, 1.0)
    vis_list = draw_vis_list(jax.random.fold_in(jax.random.fold_in(keys[11], part), 71), part)
    counts = draw_counts(jax.random.fold_in(jax.random.fold_in(keys[11], part), 71), part)
    occl = set_ends(jax.random.randint(part_keys[5], (NROWB, LIST, BS // 16, BS), 0, 65536), jax.random.fold_in(part_keys[5], 1), 0, 65535).astype(jnp.int32)
    direct = jnp.clip(jnp.exp(math.log(2.0) - 2.9957323 * jax.random.uniform(part_keys[6], (BANDS, NF), jnp.float32) ** shard_levels(part_keys[6], (BANDS, NF), ((0, 2), (1, 4)), -0.2, 0.2)), 0.1, 2.0)
    reflect = jnp.clip(0.25 + 0.65 * jax.random.uniform(part_keys[7], (BANDS, NF), jnp.float32) ** shard_levels(part_keys[7], (BANDS, NF), ((0, 2), (1, 4)), -0.2, 0.2), 0.25, 0.9)
    band_frac = jnp.clip(jnp.exp(math.log(0.2) - 2.3025851 * jax.random.uniform(keys[8], (BANDS,), jnp.float32) ** shard_levels(keys[8], (BANDS,), ((0, 2),), -0.2, 0.2)), 0.02, 0.2)
    temp = jnp.clip(0.8 + 0.40000004 * jax.random.uniform(part_keys[9], (NF,), jnp.float32) ** shard_levels(part_keys[9], (NF,), ((0, 4),), -0.2, 0.2), 0.8, 1.2)
    heat = jnp.clip(jnp.exp(math.log(0.2) - 2.3025851 * jax.random.uniform(part_keys[10], (NF,), jnp.float32) ** shard_levels(part_keys[10], (NF,), ((0, 4),), -0.2, 0.2)), 0.02, 0.2)
    return {"positions": positions, "angles": angles, "area": area, "vis_list": vis_list, "counts": counts, "occl": occl, "direct": direct, "reflect": reflect, "band_frac": band_frac, "temp": temp, "heat": heat}


def normals(angles):
    azimuth = angles[0]
    height_angle = 0.5 * angles[1]
    return jnp.stack([jnp.cos(height_angle) * jnp.cos(azimuth), jnp.cos(height_angle) * jnp.sin(azimuth), jnp.sin(height_angle)])


def block_weights(pos_row, normal_row, pos_col, normal_col, area_col, packed):
    offset_vec = pos_col[:, None, :] - pos_row[:, :, None]
    dist_sq = jnp.sum(offset_vec * offset_vec, axis=0) + area_col[None, :]
    cos_row = jnp.maximum(jnp.sum(normal_row[:, :, None] * offset_vec, axis=0), 0.0)
    cos_col = jnp.maximum(-jnp.sum(normal_col[:, None, :] * offset_vec, axis=0), 0.0)
    bit_shift = jnp.arange(16, dtype=jnp.int32)
    bit_values = jnp.bitwise_and(jnp.right_shift(packed[:, None, :], bit_shift[None, :, None]), 1)
    visible = jnp.transpose(bit_values.reshape(-1, packed.shape[1])).astype(jnp.float32)
    return visible * cos_row * cos_col * area_col[None, :] / (math.pi * dist_sq * dist_sq)


def reference(positions, angles, area, vis_list, counts, occl, direct, reflect, band_frac, temp, heat):
    normal_vec = normals(angles)
    entry_ids = jnp.arange(LIST, dtype=jnp.int32)

    def row_factors(block_id):
        first = block_id * BS
        pos_row = lax.dynamic_slice_in_dim(positions, first, BS, 1)
        normal_row = lax.dynamic_slice_in_dim(normal_vec, first, BS, 1)
        area_row = lax.dynamic_slice_in_dim(area[0], first, BS, 0)

        def single(column, packed):
            col_first = column * BS
            return block_weights(pos_row, normal_row, lax.dynamic_slice_in_dim(positions, col_first, BS, 1), lax.dynamic_slice_in_dim(normal_vec, col_first, BS, 1), lax.dynamic_slice_in_dim(area[0], col_first, BS, 0), packed)

        weights = jax.vmap(single)(vis_list[block_id], occl[block_id])
        live_mask = (entry_ids < counts[block_id]).astype(jnp.float32)
        weights = weights * live_mask[:, None, None]
        row_total = jnp.sum(weights, axis=(0, 2))
        return weights / (row_total + area_row)[None, :, None]

    def incoming_of(field_now):
        def one_row(block_id):
            factors_blk = row_factors(block_id)
            col_values = jax.vmap(lambda column: lax.dynamic_slice_in_dim(field_now, column * BS, BS, 1))(vis_list[block_id])
            return jnp.einsum("eij,ebj->bi", factors_blk, col_values, precision=lax.Precision.HIGHEST)

        pieces_out = lax.map(one_row, jnp.arange(NROWB, dtype=jnp.int32))
        return jnp.transpose(pieces_out, (1, 0, 2)).reshape(BANDS, NF)

    temp_fourth = temp * temp * temp * temp
    emitted = reflect * direct + (1.0 - reflect) * band_frac[:, None] * temp_fourth[None, :]
    radiosity = emitted
    for iteration in range(ITERS):
        incoming = incoming_of(radiosity)
        radiosity = emitted + reflect * incoming
    net_flux_part = jnp.sum((1.0 - reflect) * (direct + incoming - band_frac[:, None] * temp_fourth[None, :]), axis=0)
    return radiosity, temp + heat * net_flux_part
```

```python
import functools
import math

import jax
import jax.numpy as jnp
from jax import lax
from jax.experimental import pallas as pl
from jax.experimental.pallas import tpu as pltpu
from jax.sharding import PartitionSpec as P

ITERS = 3
MESH = pl.DeviceIdType.MESH


def split3(x):
    hi = x.astype(jnp.bfloat16).astype(jnp.float32)
    rest = x - hi
    mid = rest.astype(jnp.bfloat16).astype(jnp.float32)
    return hi, mid, rest - mid


def kernel(
    sizes,
    pos_ref, ang_ref, area_ref, vis_ref, counts_ref, occl_ref, direct_ref, reflect_ref, frac_ref, temp_ref, heat_ref,
    out_ref, newt_ref,
    geo, nrm, coef, rhs, w_hi, w_lo, words, vis_v, vis_s, last, net,
    send_sem, recv_sem, loc_sem,
    *fields,
):
    n_blk, n_band, n_sub, blocks, listed, size = sizes
    half = blocks // n_sub
    slots = listed * n_sub
    chunk = size // 16
    z = lax.axis_index("blk")
    band = lax.axis_index("band")
    sub = lax.axis_index("sub")
    peers = [lax.rem(z + d, n_blk) for d in range(1, n_blk)]
    sources = [lax.rem(z - d + n_blk, n_blk) for d in range(1, n_blk)]
    mates = [
        (lax.rem(band + d, n_band), lax.rem(sub + s, n_sub))
        for d in range(n_band) for s in range(n_sub) if d or s
    ]
    sibling = {"sub": n_sub - 1 - sub}
    started = []

    def send(src, dst, where):
        k = len(started)
        copy = pltpu.make_async_remote_copy(
            src_ref=src, dst_ref=dst, send_sem=send_sem.at[k], recv_sem=recv_sem.at[k],
            device_id=where, device_id_type=MESH,
        )
        copy.start()
        started.append(copy)
        return copy

    barrier = pltpu.get_barrier_semaphore()
    for peer in peers:
        pl.semaphore_signal(barrier, inc=1, device_id={"blk": peer}, device_id_type=MESH)
    for mate in mates:
        pl.semaphore_signal(barrier, inc=1, device_id={"band": mate[0], "sub": mate[1]}, device_id_type=MESH)

    own_words = pltpu.make_async_copy(occl_ref.at[pl.ds(sub * half, half)], words.at[sub], loc_sem.at[0])
    own_words.start()
    vis_v[sub] = vis_ref[...]

    pos = pos_ref[...]
    ang = ang_ref[...]
    azimuth = ang[0:1]
    height = 0.5 * ang[1:2]
    cos_h = jnp.cos(height)
    normal = jnp.concatenate([cos_h * jnp.cos(azimuth), cos_h * jnp.sin(azimuth), jnp.sin(height)], axis=0)
    nrm[...] = normal
    area = area_ref[...]
    scaled = normal * (area * (1.0 / math.pi))
    dist = jnp.sum(pos * pos, axis=0, keepdims=True) + area
    shift = -jnp.sum(scaled * pos, axis=0, keepdims=True)
    for b in range(blocks):
        at = z * blocks + b
        lanes = slice(b * size, (b + 1) * size)
        geo[at, 0:3, :] = pos[:, lanes]
        geo[at, 3:6, :] = scaled[:, lanes]
        geo[at, 6:7, :] = dist[:, lanes]
        geo[at, 7:8, :] = shift[:, lanes]

    pl.semaphore_wait(barrier, len(peers) + len(mates))

    mine = pl.ds(z * blocks + sub * half, half)
    geo_in = [send(geo.at[mine], geo.at[mine], {"blk": peer}) for peer in peers]
    vis_in = send(vis_v.at[sub], vis_v.at[sub], sibling)
    words_in = send(occl_ref.at[pl.ds((n_sub - 1 - sub) * half, half)], words.at[sub], sibling)

    bands = direct_ref.shape[0]
    row = lax.broadcasted_iota(jnp.int32, (bands, 1), 0)
    frac = jnp.zeros((bands, 1), jnp.float32)
    for b in range(frac_ref.shape[0]):
        frac = jnp.where(row == b, frac_ref[b], frac)
    temp = temp_ref[...]
    temp2 = temp * temp
    black = frac * (temp2 * temp2)
    reflect = reflect_ref[...]
    emitted = reflect * direct_ref[...] + (1.0 - reflect) * black
    for b in range(blocks):
        fields[0][z * blocks + b] = emitted[:, b * size:(b + 1) * size]
    field_in = [send(fields[0].at[mine], fields[0].at[mine], {"blk": peer}) for peer in peers]

    for rr in range(half):
        lanes = pl.ds(pl.multiple_of((sub * half + rr) * size, size), size)
        pos_row = pos_ref[:, lanes]
        normal_row = nrm[:, lanes]
        coef[...] = jnp.zeros_like(coef)
        coef[0:3, 0:size] = normal_row
        coef[3:6, size:2 * size] = pos_row
        coef[7:8, size:2 * size] = jnp.ones((1, size), jnp.float32)
        coef[0:3, 2 * size:3 * size] = -2.0 * pos_row
        coef[6:7, 2 * size:3 * size] = jnp.ones((1, size), jnp.float32)
        hi, mid, low = split3(coef[...])
        parts = split3(jnp.concatenate([
            -jnp.sum(pos_row * normal_row, axis=0, keepdims=True),
            jnp.zeros((1, size), jnp.float32),
            jnp.sum(pos_row * pos_row, axis=0, keepdims=True),
        ], axis=1))
        const = jnp.concatenate(list(parts) + [jnp.zeros((5, 3 * size), jnp.float32)], axis=0)
        full = jnp.concatenate([hi, mid, low, hi, mid, hi, const, jnp.zeros_like(const)], axis=0)
        rhs[rr] = full.astype(jnp.bfloat16)

    def forward(copies, place):
        passed = []
        for copy, source in zip(copies, sources):
            copy.wait_recv()
            region = place(pl.ds(source * blocks + sub * half, half))
            passed.append(send(region, region, sibling))
        return passed

    vis_in.wait_recv()
    to_smem = pltpu.make_async_copy(vis_v, vis_s, loc_sem.at[1])
    to_smem.start()
    geo_passed = forward(geo_in, lambda region: geo.at[region])
    to_smem.wait()
    own_words.wait()
    words_in.wait_recv()
    for copy in geo_passed:
        copy.wait_recv()

    bit = jnp.left_shift(1, lax.broadcasted_iota(jnp.int32, (16, 1), 0))
    geo_row = lax.broadcasted_iota(jnp.int32, (8, 1), 0)
    is_scaled = ((geo_row >= 3) & (geo_row < 6)) | (geo_row == 7)
    ones = jnp.ones((8, size), jnp.float32)

    def named(rr, e):
        return vis_s[e // listed, sub * half + rr, e % listed]

    def weights(rr):
        valid = counts_ref[sub * half + rr]

        def tile(e, total):
            live = jnp.where(e < valid, 1.0, 0.0)
            column = geo[named(rr, e)] * jnp.where(is_scaled, live, 1.0)
            hi, mid, low = split3(column)
            lhs = jnp.concatenate([hi, hi, hi, mid, mid, low, ones, jnp.zeros_like(ones)], axis=0)
            lhs = jnp.transpose(lhs).astype(jnp.bfloat16)
            side = rhs[rr]
            for q in range(chunk // 4):
                both = jnp.dot(lhs[q * 64:(q + 1) * 64], side, preferred_element_type=jnp.float32)
                for k in range(4):
                    word = words[e // listed, rr, e % listed, pl.ds(q * 4 + k, 1), :]
                    seen = jnp.bitwise_and(word, bit) != 0
                    lines = slice(k * 16, (k + 1) * 16)
                    cos_row = jnp.where(seen, jnp.maximum(both[lines, 0:size], 0.0), 0.0)
                    cos_col = jnp.maximum(both[lines, size:2 * size], 0.0)
                    square = both[lines, 2 * size:3 * size]
                    square = square * square
                    inverse = pl.reciprocal(square, approx=True)
                    inverse = inverse * (2.0 - square * inverse)
                    w = (cos_row * cos_col) * inverse
                    total = total + (w[0:8] + w[8:16])
                    top = w.astype(jnp.bfloat16)
                    at = pl.ds(pl.multiple_of(e * size, size) + (q * 64 + k * 16), 16)
                    w_hi[rr, at, :] = top
                    w_lo[rr, at, :] = (w - top.astype(jnp.float32)).astype(jnp.bfloat16)
            return total

        total = lax.fori_loop(0, slots, tile, jnp.zeros((8, size), jnp.float32))
        return jnp.sum(total, axis=0, keepdims=True)

    totals = []
    arrived = None
    for rr in range(half):
        totals.append(weights(rr))
        if arrived is None:
            arrived = forward(field_in, lambda region: fields[0].at[region])

    inverse_denom = []
    for rr in range(half):
        lanes = pl.ds(pl.multiple_of((sub * half + rr) * size, size), size)
        inverse_denom.append(1.0 / (totals[rr] + area_ref[:, lanes]))

    waiting = arrived
    for step in range(ITERS):
        for copy in waiting:
            copy.wait_recv()
        waiting, hops = [], []
        for rr in range(half):
            field = jnp.concatenate([fields[step][named(rr, e)] for e in range(slots)], axis=1)
            top = field.astype(jnp.bfloat16).astype(jnp.float32)
            both = jnp.concatenate([top, field - top], axis=0).astype(jnp.bfloat16)
            first = jnp.dot(both, w_hi[rr], preferred_element_type=jnp.float32)
            second = jnp.dot(top.astype(jnp.bfloat16), w_lo[rr], preferred_element_type=jnp.float32)
            incoming = (first[0:bands] + first[bands:] + second) * inverse_denom[rr]
            lanes = pl.ds(pl.multiple_of((sub * half + rr) * size, size), size)
            own_reflect = reflect_ref[:, lanes]
            value = fields[0][z * blocks + sub * half + rr] + own_reflect * incoming
            if step < ITERS - 1:
                at = z * blocks + sub * half + rr
                fields[step + 1][at] = value
                region = fields[step + 1].at[pl.ds(at, 1)]
                for peer, source in zip(peers, sources):
                    hops.append((send(region, region, {"blk": peer}), source * blocks + sub * half + rr))
                waiting.append(send(region, region, sibling))
            else:
                own_temp = temp_ref[:, lanes]
                own_temp2 = own_temp * own_temp
                gain = (1.0 - own_reflect) * (
                    direct_ref[:, lanes] + incoming - frac * (own_temp2 * own_temp2)
                )
                last[sub * half + rr] = value
                region = last.at[pl.ds(sub * half + rr, 1)]
                waiting.append(send(region, region, sibling))
                net[band, sub, rr:rr + 1, :] = jnp.sum(gain, axis=0, keepdims=True)
        for copy, at in hops:
            copy.wait_recv()
            region = fields[step + 1].at[pl.ds(at, 1)]
            waiting.append(send(region, region, sibling))

    for mate in mates:
        waiting.append(send(net.at[band, sub], net.at[band, sub], {"band": mate[0], "sub": mate[1]}))
    for copy in waiting:
        copy.wait_recv()
    for b in range(blocks):
        lanes = slice(b * size, (b + 1) * size)
        out_ref[:, lanes] = last[b]
        flux = net[0, b // half, b % half:b % half + 1, :]
        for other in range(1, n_band):
            flux = flux + net[other, b // half, b % half:b % half + 1, :]
        newt_ref[:, lanes] = temp_ref[:, lanes] + heat_ref[:, lanes] * flux
    for copy in started:
        copy.wait_send()


def local(axes, positions, angles, area, vis_list, counts, occl, direct, reflect, band_frac, temp, heat):
    n_blk, n_band, n_sub = axes
    size = occl.shape[3]
    blocks, listed = vis_list.shape
    half = blocks // n_sub
    rows = positions.shape[1]
    band_count = direct.shape[0]
    bands = -(-band_count // 8) * 8
    if bands != band_count:
        direct = jnp.pad(direct, ((0, bands - band_count), (0, 0)))
        reflect = jnp.pad(reflect, ((0, bands - band_count), (0, 0)), constant_values=1.0)
    total_blocks = n_blk * blocks
    slots = listed * n_sub
    copies = (
        (n_blk - 1) * 4 + 2 + (ITERS - 1) * half * (2 * (n_blk - 1) + 1) + half + n_band * n_sub - 1
    )
    vmem = pl.BlockSpec(memory_space=pltpu.VMEM)
    smem = pl.BlockSpec(memory_space=pltpu.SMEM)
    out, new_temp = pl.pallas_call(
        functools.partial(kernel, (n_blk, n_band, n_sub, blocks, listed, size)),
        out_shape=(
            jax.ShapeDtypeStruct((bands, rows), jnp.float32),
            jax.ShapeDtypeStruct((1, rows), jnp.float32),
        ),
        in_specs=[vmem, vmem, vmem, vmem, smem, pl.BlockSpec(memory_space=pl.ANY), vmem, vmem, smem, vmem, vmem],
        out_specs=(vmem, vmem),
        scratch_shapes=[
            pltpu.VMEM((total_blocks, 8, size), jnp.float32),
            pltpu.VMEM((3, rows), jnp.float32),
            pltpu.VMEM((8, 3 * size), jnp.float32),
            pltpu.VMEM((half, 64, 3 * size), jnp.bfloat16),
            pltpu.VMEM((half, slots * size, size), jnp.bfloat16),
            pltpu.VMEM((half, slots * size, size), jnp.bfloat16),
            pltpu.VMEM((n_sub, half, listed, size // 16, size), jnp.int32),
            pltpu.VMEM((n_sub, blocks, listed), jnp.int32),
            pltpu.SMEM((n_sub, blocks, listed), jnp.int32),
            pltpu.VMEM((blocks, bands, size), jnp.float32),
            pltpu.VMEM((n_band, n_sub, half, size), jnp.float32),
            pltpu.SemaphoreType.DMA((copies,)),
            pltpu.SemaphoreType.DMA((copies,)),
            pltpu.SemaphoreType.DMA((2,)),
        ]
        + [pltpu.VMEM((total_blocks, bands, size), jnp.float32)] * ITERS,
        compiler_params=pltpu.CompilerParams(
            collective_id=0, has_side_effects=True, vmem_limit_bytes=40 * 1024 * 1024
        ),
    )(positions, angles, area, vis_list, counts, occl, direct, reflect, band_frac, temp[None, :], heat[None, :])
    return out[:band_count], new_temp.reshape(rows)


def solution(mesh):
    placed = (
        P(None, ("city", "blk")),
        P(None, ("city", "blk")),
        P(None, ("city", "blk")),
        P(("city", "blk"), "sub"),
        P(("city", "blk")),
        P(("city", "blk"), "sub", None, None),
        P("band", ("city", "blk")),
        P("band", ("city", "blk")),
        P("band"),
        P(("city", "blk")),
        P(("city", "blk")),
    )
    axes = (mesh.shape["blk"], mesh.shape["band"], mesh.shape["sub"])
    return jax.shard_map(
        functools.partial(local, axes),
        mesh=mesh,
        in_specs=placed,
        out_specs=(P("band", ("city", "blk")), P(("city", "blk"))),
        check_vma=False,
    )
```

```python
import functools
import math

import jax
import jax.numpy as jnp
from jax import lax
from jax.experimental import pallas as pl
from jax.experimental.pallas import tpu as pltpu
from jax.sharding import PartitionSpec as P

ITERS = 3
MESH = pl.DeviceIdType.MESH


def split3(x):
    hi = x.astype(jnp.bfloat16).astype(jnp.float32)
    rest = x - hi
    mid = rest.astype(jnp.bfloat16).astype(jnp.float32)
    return hi, mid, rest - mid


def kernel(
    sizes,
    pos_in, ang_in, area_in, vis_ref, counts_in, occl_ref, direct_in, reflect_in, frac_in, temp_in, heat_in,
    out_ref, newt_ref,
    pos_ref, ang_ref, area_ref, counts_ref, direct_ref, reflect_ref, frac_ref, temp_ref, heat_ref,
    geo, nrm, coef, rhs, w_hi, w_lo, words, vis_v, vis_s, last, net,
    send_sem, recv_sem, loc_sem,
    *fields,
):
    n_blk, n_band, n_sub, blocks, listed, size = sizes
    half = blocks // n_sub
    slots = listed * n_sub
    chunk = size // 16
    z = lax.axis_index("blk")
    band = lax.axis_index("band")
    sub = lax.axis_index("sub")
    peers = [lax.rem(z + d, n_blk) for d in range(1, n_blk)]
    sources = [lax.rem(z - d + n_blk, n_blk) for d in range(1, n_blk)]
    mates = [
        (lax.rem(band + d, n_band), lax.rem(sub + s, n_sub))
        for d in range(n_band) for s in range(n_sub) if d or s
    ]
    sibling = {"sub": n_sub - 1 - sub}
    started = []

    def send(src, dst, where):
        k = len(started)
        copy = pltpu.make_async_remote_copy(
            src_ref=src, dst_ref=dst, send_sem=send_sem.at[k], recv_sem=recv_sem.at[k],
            device_id=where, device_id_type=MESH,
        )
        copy.start()
        started.append(copy)
        return copy

    loads = []

    def load(src, dst):
        copy = pltpu.make_async_copy(src, dst, loc_sem.at[len(loads)])
        copy.start()
        loads.append(copy)
        return copy

    shape_in = [load(ang_in, ang_ref), load(pos_in, pos_ref), load(area_in, area_ref)]
    vis_load = load(vis_ref, vis_v.at[sub])
    field_loads = [
        load(frac_in, frac_ref), load(temp_in, temp_ref), load(direct_in, direct_ref), load(reflect_in, reflect_ref)
    ]
    late_loads = [
        load(occl_ref.at[pl.ds(sub * half, half)], words.at[sub]), load(counts_in, counts_ref), load(heat_in, heat_ref)
    ]

    barrier = pltpu.get_barrier_semaphore()
    for peer in peers:
        pl.semaphore_signal(barrier, inc=1, device_id={"blk": peer}, device_id_type=MESH)
    for mate in mates:
        pl.semaphore_signal(barrier, inc=1, device_id={"band": mate[0], "sub": mate[1]}, device_id_type=MESH)


    for copy in shape_in:
        copy.wait()
    pos = pos_ref[...]
    ang = ang_ref[...]
    ang = jnp.concatenate([ang[:, b * size:(b + 1) * size] for b in range(blocks)], axis=0)
    odd = lax.broadcasted_iota(jnp.int32, ang.shape, 0) % 2 == 1
    ang = jnp.where(odd, 0.5 * ang, ang)
    cos, sin = jnp.cos(ang), jnp.sin(ang)
    normal = []
    for b in range(blocks):
        cos_h = cos[2 * b + 1:2 * b + 2]
        normal.append(jnp.concatenate(
            [cos_h * cos[2 * b:2 * b + 1], cos_h * sin[2 * b:2 * b + 1], sin[2 * b + 1:2 * b + 2]], axis=0
        ))
    normal = jnp.concatenate(normal, axis=1)
    nrm[...] = normal
    area = area_ref[...]
    scaled = normal * (area * (1.0 / math.pi))
    dist = jnp.sum(pos * pos, axis=0, keepdims=True) + area
    shift = -jnp.sum(scaled * pos, axis=0, keepdims=True)
    for b in range(blocks):
        at = z * blocks + b
        lanes = slice(b * size, (b + 1) * size)
        geo[at, 0:3, :] = pos[:, lanes]
        geo[at, 3:6, :] = scaled[:, lanes]
        geo[at, 6:7, :] = dist[:, lanes]
        geo[at, 7:8, :] = shift[:, lanes]

    for copy in field_loads:
        copy.wait()
    bands = direct_ref.shape[0]
    row = lax.broadcasted_iota(jnp.int32, (bands, 1), 0)
    frac = jnp.zeros((bands, 1), jnp.float32)
    for b in range(frac_ref.shape[0]):
        frac = jnp.where(row == b, frac_ref[b], frac)
    temp = temp_ref[...]
    temp2 = temp * temp
    black = frac * (temp2 * temp2)
    reflect = reflect_ref[...]
    emitted = reflect * direct_ref[...] + (1.0 - reflect) * black
    for b in range(blocks):
        fields[0][z * blocks + b] = emitted[:, b * size:(b + 1) * size]
    for rr in range(half):
        lanes = pl.ds(pl.multiple_of((sub * half + rr) * size, size), size)
        pos_row = pos_ref[:, lanes]
        normal_row = nrm[:, lanes]
        coef[...] = jnp.zeros_like(coef)
        coef[0:3, 0:size] = normal_row
        coef[3:6, size:2 * size] = pos_row
        coef[7:8, size:2 * size] = jnp.ones((1, size), jnp.float32)
        coef[0:3, 2 * size:3 * size] = -2.0 * pos_row
        coef[6:7, 2 * size:3 * size] = jnp.ones((1, size), jnp.float32)
        hi, mid, low = split3(coef[...])
        parts = split3(jnp.concatenate([
            -jnp.sum(pos_row * normal_row, axis=0, keepdims=True),
            jnp.zeros((1, size), jnp.float32),
            jnp.sum(pos_row * pos_row, axis=0, keepdims=True),
        ], axis=1))
        const = jnp.concatenate(list(parts) + [jnp.zeros((5, 3 * size), jnp.float32)], axis=0)
        full = jnp.concatenate([hi, mid, low, hi, mid, hi, const, jnp.zeros_like(const)], axis=0)
        rhs[rr] = full.astype(jnp.bfloat16)

    pl.semaphore_wait(barrier, len(peers) + len(mates))

    mine = pl.ds(z * blocks + sub * half, half)
    geo_in = [send(geo.at[mine], geo.at[mine], {"blk": peer}) for peer in peers]
    vis_load.wait()
    vis_in = send(vis_v.at[sub], vis_v.at[sub], sibling)
    words_in = send(occl_ref.at[pl.ds((n_sub - 1 - sub) * half, half)], words.at[sub], sibling)

    field_in = [send(fields[0].at[mine], fields[0].at[mine], {"blk": peer}) for peer in peers]

    def forward(copies, place):
        passed = []
        for copy, source in zip(copies, sources):
            copy.wait_recv()
            region = place(pl.ds(source * blocks + sub * half, half))
            passed.append(send(region, region, sibling))
        return passed

    vis_in.wait_recv()
    to_smem = pltpu.make_async_copy(vis_v, vis_s, loc_sem.at[len(loads)])
    to_smem.start()
    geo_passed = forward(geo_in, lambda region: geo.at[region])
    to_smem.wait()
    for copy in late_loads:
        copy.wait()
    words_in.wait_recv()
    for copy in geo_passed:
        copy.wait_recv()

    bit = jnp.left_shift(1, lax.broadcasted_iota(jnp.int32, (16, 1), 0))
    geo_row = lax.broadcasted_iota(jnp.int32, (8, 1), 0)
    is_scaled = ((geo_row >= 3) & (geo_row < 6)) | (geo_row == 7)
    ones = jnp.ones((8, size), jnp.float32)

    def named(rr, e):
        return vis_s[e // listed, sub * half + rr, e % listed]

    def weights(rr):
        valid = counts_ref[sub * half + rr]

        def tile(e, total):
            live = jnp.where(e < valid, 1.0, 0.0)
            column = geo[named(rr, e)] * jnp.where(is_scaled, live, 1.0)
            hi, mid, low = split3(column)
            lhs = jnp.concatenate([hi, hi, hi, mid, mid, low, ones, jnp.zeros_like(ones)], axis=0)
            lhs = jnp.transpose(lhs).astype(jnp.bfloat16)
            side = rhs[rr]
            for q in range(chunk // 4):
                both = jnp.dot(lhs[q * 64:(q + 1) * 64], side, preferred_element_type=jnp.float32)
                for k in range(4):
                    word = words[e // listed, rr, e % listed, pl.ds(q * 4 + k, 1), :]
                    seen = jnp.bitwise_and(word, bit) != 0
                    lines = slice(k * 16, (k + 1) * 16)
                    cos_row = jnp.where(seen, jnp.maximum(both[lines, 0:size], 0.0), 0.0)
                    cos_col = jnp.maximum(both[lines, size:2 * size], 0.0)
                    square = both[lines, 2 * size:3 * size]
                    square = square * square
                    inverse = pl.reciprocal(square, approx=True)
                    inverse = inverse * (2.0 - square * inverse)
                    w = (cos_row * cos_col) * inverse
                    total = total + (w[0:8] + w[8:16])
                    top = w.astype(jnp.bfloat16)
                    at = pl.ds(pl.multiple_of(e * size, size) + (q * 64 + k * 16), 16)
                    w_hi[rr, at, :] = top
                    w_lo[rr, at, :] = (w - top.astype(jnp.float32)).astype(jnp.bfloat16)
            return total

        total = lax.fori_loop(0, slots, tile, jnp.zeros((8, size), jnp.float32), unroll=4)
        return jnp.sum(total, axis=0, keepdims=True)

    totals = []
    arrived = None
    for rr in range(half):
        totals.append(weights(rr))
        if arrived is None:
            arrived = forward(field_in, lambda region: fields[0].at[region])

    inverse_denom = []
    for rr in range(half):
        lanes = pl.ds(pl.multiple_of((sub * half + rr) * size, size), size)
        inverse_denom.append(1.0 / (totals[rr] + area_ref[:, lanes]))

    waiting = arrived
    for step in range(ITERS):
        for copy in waiting:
            copy.wait_recv()
        waiting, hops = [], []
        for rr in range(half):
            field = jnp.concatenate([fields[step][named(rr, e)] for e in range(slots)], axis=1)
            top = field.astype(jnp.bfloat16).astype(jnp.float32)
            both = jnp.concatenate([top, field - top], axis=0).astype(jnp.bfloat16)
            first = jnp.dot(both, w_hi[rr], preferred_element_type=jnp.float32)
            second = jnp.dot(top.astype(jnp.bfloat16), w_lo[rr], preferred_element_type=jnp.float32)
            incoming = (first[0:bands] + first[bands:] + second) * inverse_denom[rr]
            lanes = pl.ds(pl.multiple_of((sub * half + rr) * size, size), size)
            own_reflect = reflect_ref[:, lanes]
            value = fields[0][z * blocks + sub * half + rr] + own_reflect * incoming
            if step < ITERS - 1:
                at = z * blocks + sub * half + rr
                fields[step + 1][at] = value
                region = fields[step + 1].at[pl.ds(at, 1)]
                for peer, source in zip(peers, sources):
                    hops.append((send(region, region, {"blk": peer}), source * blocks + sub * half + rr))
                waiting.append(send(region, region, sibling))
            else:
                own_temp = temp_ref[:, lanes]
                own_temp2 = own_temp * own_temp
                gain = (1.0 - own_reflect) * (
                    direct_ref[:, lanes] + incoming - frac * (own_temp2 * own_temp2)
                )
                last[sub * half + rr] = value
                region = last.at[pl.ds(sub * half + rr, 1)]
                waiting.append(send(region, region, sibling))
                net[band, sub, rr:rr + 1, :] = jnp.sum(gain, axis=0, keepdims=True)
        for copy, at in hops:
            copy.wait_recv()
            region = fields[step + 1].at[pl.ds(at, 1)]
            waiting.append(send(region, region, sibling))

    for mate in mates:
        waiting.append(send(net.at[band, sub], net.at[band, sub], {"band": mate[0], "sub": mate[1]}))
    for copy in waiting:
        copy.wait_recv()
    for b in range(blocks):
        lanes = slice(b * size, (b + 1) * size)
        out_ref[:, lanes] = last[b]
        flux = net[0, b // half, b % half:b % half + 1, :]
        for other in range(1, n_band):
            flux = flux + net[other, b // half, b % half:b % half + 1, :]
        newt_ref[:, lanes] = temp_ref[:, lanes] + heat_ref[:, lanes] * flux
    for copy in started:
        copy.wait_send()


def local(axes, positions, angles, area, vis_list, counts, occl, direct, reflect, band_frac, temp, heat):
    n_blk, n_band, n_sub = axes
    size = occl.shape[3]
    blocks, listed = vis_list.shape
    half = blocks // n_sub
    rows = positions.shape[1]
    band_count = direct.shape[0]
    bands = -(-band_count // 8) * 8
    if bands != band_count:
        direct = jnp.pad(direct, ((0, bands - band_count), (0, 0)))
        reflect = jnp.pad(reflect, ((0, bands - band_count), (0, 0)), constant_values=1.0)
    total_blocks = n_blk * blocks
    slots = listed * n_sub
    copies = (
        (n_blk - 1) * 4 + 2 + (ITERS - 1) * half * (2 * (n_blk - 1) + 1) + half + n_band * n_sub - 1
    )
    vmem = pl.BlockSpec(memory_space=pltpu.VMEM)
    hbm = pl.BlockSpec(memory_space=pltpu.HBM)
    out, new_temp = pl.pallas_call(
        functools.partial(kernel, (n_blk, n_band, n_sub, blocks, listed, size)),
        out_shape=(
            jax.ShapeDtypeStruct((bands, rows), jnp.float32),
            jax.ShapeDtypeStruct((1, rows), jnp.float32),
        ),
        in_specs=[hbm] * 11,
        out_specs=(vmem, vmem),
        scratch_shapes=[
            pltpu.VMEM(positions.shape, jnp.float32),
            pltpu.VMEM(angles.shape, jnp.float32),
            pltpu.VMEM(area.shape, jnp.float32),
            pltpu.SMEM(counts.shape, jnp.int32),
            pltpu.VMEM(direct.shape, jnp.float32),
            pltpu.VMEM(reflect.shape, jnp.float32),
            pltpu.SMEM(band_frac.shape, jnp.float32),
            pltpu.VMEM((1, rows), jnp.float32),
            pltpu.VMEM((1, rows), jnp.float32),
            pltpu.VMEM((total_blocks, 8, size), jnp.float32),
            pltpu.VMEM((3, rows), jnp.float32),
            pltpu.VMEM((8, 3 * size), jnp.float32),
            pltpu.VMEM((half, 64, 3 * size), jnp.bfloat16),
            pltpu.VMEM((half, slots * size, size), jnp.bfloat16),
            pltpu.VMEM((half, slots * size, size), jnp.bfloat16),
            pltpu.VMEM((n_sub, half, listed, size // 16, size), jnp.int32),
            pltpu.VMEM((n_sub, blocks, listed), jnp.int32),
            pltpu.SMEM((n_sub, blocks, listed), jnp.int32),
            pltpu.VMEM((blocks, bands, size), jnp.float32),
            pltpu.VMEM((n_band, n_sub, half, size), jnp.float32),
            pltpu.SemaphoreType.DMA((copies,)),
            pltpu.SemaphoreType.DMA((copies,)),
            pltpu.SemaphoreType.DMA((12,)),
        ]
        + [pltpu.VMEM((total_blocks, bands, size), jnp.float32)] * ITERS,
        compiler_params=pltpu.CompilerParams(
            collective_id=0, has_side_effects=True, vmem_limit_bytes=60 * 1024 * 1024
        ),
    )(positions, angles, area, vis_list, counts, occl, direct, reflect, band_frac, temp[None, :], heat[None, :])
    return out[:band_count], new_temp.reshape(rows)


def solution(mesh):
    placed = (
        P(None, ("city", "blk")),
        P(None, ("city", "blk")),
        P(None, ("city", "blk")),
        P(("city", "blk"), "sub"),
        P(("city", "blk")),
        P(("city", "blk"), "sub", None, None),
        P("band", ("city", "blk")),
        P("band", ("city", "blk")),
        P("band"),
        P(("city", "blk")),
        P(("city", "blk")),
    )
    axes = (mesh.shape["blk"], mesh.shape["band"], mesh.shape["sub"])
    return jax.shard_map(
        functools.partial(local, axes),
        mesh=mesh,
        in_specs=placed,
        out_specs=(P("band", ("city", "blk")), P(("city", "blk"))),
        check_vma=False,
    )
```

```python
import functools
import math

import jax
import jax.numpy as jnp
from jax import lax
from jax.experimental import pallas as pl
from jax.experimental.pallas import tpu as pltpu
from jax.sharding import PartitionSpec as P

ITERS = 3
MESH = pl.DeviceIdType.MESH


def split3(x):
    hi = x.astype(jnp.bfloat16).astype(jnp.float32)
    rest = x - hi
    mid = rest.astype(jnp.bfloat16).astype(jnp.float32)
    return hi, mid, rest - mid


def kernel(
    sizes,
    pos_in, ang_in, area_in, vis_ref, counts_in, occl_ref, direct_in, reflect_in, frac_in, temp_in, heat_in,
    out_ref, newt_ref,
    pos_ref, ang_ref, area_ref, counts_ref, direct_ref, reflect_ref, frac_ref, temp_ref, heat_ref,
    geo, nrm, coef, rhs, w_hi, w_lo, words, vis_v, vis_s, last, net,
    send_sem, recv_sem, loc_sem,
    *fields,
):
    n_blk, n_band, n_sub, blocks, listed, size = sizes
    half = blocks // n_sub
    slots = listed * n_sub
    chunk = size // 16
    z = lax.axis_index("blk")
    band = lax.axis_index("band")
    sub = lax.axis_index("sub")
    peers = [lax.rem(z + d, n_blk) for d in range(1, n_blk)]
    sources = [lax.rem(z - d + n_blk, n_blk) for d in range(1, n_blk)]
    mates = [
        (lax.rem(band + d, n_band), lax.rem(sub + s, n_sub))
        for d in range(n_band) for s in range(n_sub) if d or s
    ]
    sibling = {"sub": n_sub - 1 - sub}
    started = []

    def send(src, dst, where):
        k = len(started)
        copy = pltpu.make_async_remote_copy(
            src_ref=src, dst_ref=dst, send_sem=send_sem.at[k], recv_sem=recv_sem.at[k],
            device_id=where, device_id_type=MESH,
        )
        copy.start()
        started.append(copy)
        return copy

    loads = []

    def load(src, dst):
        copy = pltpu.make_async_copy(src, dst, loc_sem.at[len(loads)])
        copy.start()
        loads.append(copy)
        return copy

    shape_in = [load(ang_in, ang_ref), load(pos_in, pos_ref), load(area_in, area_ref)]
    vis_load = load(vis_ref, vis_v.at[sub])
    field_loads = [
        load(frac_in, frac_ref), load(temp_in, temp_ref), load(direct_in, direct_ref), load(reflect_in, reflect_ref)
    ]
    late_loads = [
        load(occl_ref.at[pl.ds(sub * half, half)], words.at[sub]), load(counts_in, counts_ref), load(heat_in, heat_ref)
    ]

    barrier = pltpu.get_barrier_semaphore()
    for peer in peers:
        pl.semaphore_signal(barrier, inc=1, device_id={"blk": peer}, device_id_type=MESH)
    for mate in mates:
        pl.semaphore_signal(barrier, inc=1, device_id={"band": mate[0], "sub": mate[1]}, device_id_type=MESH)


    for copy in shape_in:
        copy.wait()
    pos = pos_ref[...]
    ang = ang_ref[...]
    ang = jnp.concatenate([ang[:, b * size:(b + 1) * size] for b in range(blocks)], axis=0)
    odd = lax.broadcasted_iota(jnp.int32, ang.shape, 0) % 2 == 1
    ang = jnp.where(odd, 0.5 * ang, ang)
    cos, sin = jnp.cos(ang), jnp.sin(ang)
    normal = []
    for b in range(blocks):
        cos_h = cos[2 * b + 1:2 * b + 2]
        normal.append(jnp.concatenate(
            [cos_h * cos[2 * b:2 * b + 1], cos_h * sin[2 * b:2 * b + 1], sin[2 * b + 1:2 * b + 2]], axis=0
        ))
    normal = jnp.concatenate(normal, axis=1)
    nrm[...] = normal
    area = area_ref[...]
    scaled = normal * (area * (1.0 / math.pi))
    dist = jnp.sum(pos * pos, axis=0, keepdims=True) + area
    shift = -jnp.sum(scaled * pos, axis=0, keepdims=True)
    for b in range(blocks):
        at = z * blocks + b
        lanes = slice(b * size, (b + 1) * size)
        geo[at, 0:3, :] = pos[:, lanes]
        geo[at, 3:6, :] = scaled[:, lanes]
        geo[at, 6:7, :] = dist[:, lanes]
        geo[at, 7:8, :] = shift[:, lanes]

    for copy in field_loads:
        copy.wait()
    bands = direct_ref.shape[0]
    row = lax.broadcasted_iota(jnp.int32, (bands, 1), 0)
    frac = jnp.zeros((bands, 1), jnp.float32)
    for b in range(frac_ref.shape[0]):
        frac = jnp.where(row == b, frac_ref[b], frac)
    temp = temp_ref[...]
    temp2 = temp * temp
    black = frac * (temp2 * temp2)
    reflect = reflect_ref[...]
    emitted = reflect * direct_ref[...] + (1.0 - reflect) * black
    for b in range(blocks):
        fields[0][z * blocks + b] = emitted[:, b * size:(b + 1) * size]
    for rr in range(half):
        lanes = pl.ds(pl.multiple_of((sub * half + rr) * size, size), size)
        pos_row = pos_ref[:, lanes]
        normal_row = nrm[:, lanes]
        coef[...] = jnp.zeros_like(coef)
        coef[0:3, 0:size] = normal_row
        coef[3:6, size:2 * size] = pos_row
        coef[7:8, size:2 * size] = jnp.ones((1, size), jnp.float32)
        coef[0:3, 2 * size:3 * size] = -2.0 * pos_row
        coef[6:7, 2 * size:3 * size] = jnp.ones((1, size), jnp.float32)
        hi, mid, low = split3(coef[...])
        parts = split3(jnp.concatenate([
            -jnp.sum(pos_row * normal_row, axis=0, keepdims=True),
            jnp.zeros((1, size), jnp.float32),
            jnp.sum(pos_row * pos_row, axis=0, keepdims=True),
        ], axis=1))
        const = jnp.concatenate(list(parts) + [jnp.zeros((5, 3 * size), jnp.float32)], axis=0)
        full = jnp.concatenate([hi, mid, low, hi, mid, hi, const, jnp.zeros_like(const)], axis=0)
        rhs[rr] = full.astype(jnp.bfloat16)

    pl.semaphore_wait(barrier, len(peers) + len(mates))

    mine = pl.ds(z * blocks + sub * half, half)
    geo_in = [send(geo.at[mine], geo.at[mine], {"blk": peer}) for peer in peers]
    vis_load.wait()
    vis_in = send(vis_v.at[sub], vis_v.at[sub], sibling)
    words_in = send(occl_ref.at[pl.ds((n_sub - 1 - sub) * half, half)], words.at[sub], sibling)

    field_in = [send(fields[0].at[mine], fields[0].at[mine], {"blk": peer}) for peer in peers]

    def forward(copies, place):
        passed = []
        for copy, source in zip(copies, sources):
            copy.wait_recv()
            region = place(pl.ds(source * blocks + sub * half, half))
            passed.append(send(region, region, sibling))
        return passed

    vis_in.wait_recv()
    to_smem = pltpu.make_async_copy(vis_v, vis_s, loc_sem.at[len(loads)])
    to_smem.start()
    geo_passed = forward(geo_in, lambda region: geo.at[region])
    to_smem.wait()
    for copy in late_loads:
        copy.wait()
    words_in.wait_recv()
    for copy in geo_passed:
        copy.wait_recv()

    bit = jnp.left_shift(1, lax.broadcasted_iota(jnp.int32, (16, 1), 0))
    geo_row = lax.broadcasted_iota(jnp.int32, (8, 1), 0)
    is_scaled = ((geo_row >= 3) & (geo_row < 6)) | (geo_row == 7)
    ones = jnp.ones((8, size), jnp.float32)

    def named(rr, e):
        return vis_s[e // listed, sub * half + rr, e % listed]

    def weights(rr):
        valid = counts_ref[sub * half + rr]

        def tile(e, total):
            live = jnp.where(e < valid, 1.0, 0.0)
            column = geo[named(rr, e)] * jnp.where(is_scaled, live, 1.0)
            hi, mid, low = split3(column)
            lhs = jnp.concatenate([hi, hi, hi, mid, mid, low, ones, jnp.zeros_like(ones)], axis=0)
            lhs = jnp.transpose(lhs).astype(jnp.bfloat16)
            side = rhs[rr]
            for q in range(chunk // 4):
                both = jnp.dot(lhs[q * 64:(q + 1) * 64], side, preferred_element_type=jnp.float32)
                for k in range(4):
                    word = words[e // listed, rr, e % listed, pl.ds(q * 4 + k, 1), :]
                    seen = jnp.bitwise_and(word, bit) != 0
                    lines = slice(k * 16, (k + 1) * 16)
                    cos_row = jnp.where(seen, jnp.maximum(both[lines, 0:size], 0.0), 0.0)
                    cos_col = jnp.maximum(both[lines, size:2 * size], 0.0)
                    square = both[lines, 2 * size:3 * size]
                    square = square * square
                    inverse = pl.reciprocal(square, approx=True)
                    inverse = inverse * (2.0 - square * inverse)
                    w = (cos_row * cos_col) * inverse
                    total = total + (w[0:8] + w[8:16])
                    top = w.astype(jnp.bfloat16)
                    at = pl.ds(pl.multiple_of(e * size, size) + (q * 64 + k * 16), 16)
                    w_hi[rr, at, :] = top
                    w_lo[rr, at, :] = (w - top.astype(jnp.float32)).astype(jnp.bfloat16)
            return total

        total = lax.fori_loop(0, slots, tile, jnp.zeros((8, size), jnp.float32), unroll=4)
        return jnp.sum(total, axis=0, keepdims=True)

    totals = []
    arrived = None
    for rr in range(half):
        totals.append(weights(rr))
        if arrived is None:
            arrived = forward(field_in, lambda region: fields[0].at[region])

    inverse_denom = []
    for rr in range(half):
        lanes = pl.ds(pl.multiple_of((sub * half + rr) * size, size), size)
        inverse_denom.append(1.0 / (totals[rr] + area_ref[:, lanes]))

    waiting = arrived
    for step in range(ITERS):
        for copy in waiting:
            copy.wait_recv()
        waiting, hops = [], []
        for rr in range(half):
            field = jnp.concatenate([fields[step][named(rr, e)] for e in range(slots)], axis=1)
            top = field.astype(jnp.bfloat16).astype(jnp.float32)
            both = jnp.concatenate([top, field - top], axis=0).astype(jnp.bfloat16)
            first = jnp.dot(both, w_hi[rr], preferred_element_type=jnp.float32)
            second = jnp.dot(top.astype(jnp.bfloat16), w_lo[rr], preferred_element_type=jnp.float32)
            incoming = (first[0:bands] + first[bands:] + second) * inverse_denom[rr]
            lanes = pl.ds(pl.multiple_of((sub * half + rr) * size, size), size)
            own_reflect = reflect_ref[:, lanes]
            value = fields[0][z * blocks + sub * half + rr] + own_reflect * incoming
            if step < ITERS - 1:
                at = z * blocks + sub * half + rr
                fields[step + 1][at] = value
                region = fields[step + 1].at[pl.ds(at, 1)]
                for peer, source in zip(peers, sources):
                    hops.append((send(region, region, {"blk": peer}), source * blocks + sub * half + rr))
                waiting.append(send(region, region, sibling))
            else:
                own_temp = temp_ref[:, lanes]
                own_temp2 = own_temp * own_temp
                gain = (1.0 - own_reflect) * (
                    direct_ref[:, lanes] + incoming - frac * (own_temp2 * own_temp2)
                )
                net[band, sub, rr:rr + 1, :] = jnp.sum(gain, axis=0, keepdims=True)
                if rr == half - 1:
                    for mate in mates:
                        waiting.append(
                            send(net.at[band, sub], net.at[band, sub], {"band": mate[0], "sub": mate[1]})
                        )
                last[sub * half + rr] = value
                region = last.at[pl.ds(sub * half + rr, 1)]
                waiting.append(send(region, region, sibling))
        for copy, at in hops:
            copy.wait_recv()
            region = fields[step + 1].at[pl.ds(at, 1)]
            waiting.append(send(region, region, sibling))

    for copy in waiting:
        copy.wait_recv()
    for b in range(blocks):
        lanes = slice(b * size, (b + 1) * size)
        out_ref[:, lanes] = last[b]
        flux = net[0, b // half, b % half:b % half + 1, :]
        for other in range(1, n_band):
            flux = flux + net[other, b // half, b % half:b % half + 1, :]
        newt_ref[:, lanes] = temp_ref[:, lanes] + heat_ref[:, lanes] * flux
    for copy in started:
        copy.wait_send()


def finish(out_in, newt_in, out_ref, newt_ref):
    out_ref[...] = out_in[...]
    newt_ref[...] = newt_in[...]


def local(axes, positions, angles, area, vis_list, counts, occl, direct, reflect, band_frac, temp, heat):
    n_blk, n_band, n_sub = axes
    size = occl.shape[3]
    blocks, listed = vis_list.shape
    half = blocks // n_sub
    rows = positions.shape[1]
    band_count = direct.shape[0]
    bands = -(-band_count // 8) * 8
    if bands != band_count:
        direct = jnp.pad(direct, ((0, bands - band_count), (0, 0)))
        reflect = jnp.pad(reflect, ((0, bands - band_count), (0, 0)), constant_values=1.0)
    total_blocks = n_blk * blocks
    slots = listed * n_sub
    copies = (
        (n_blk - 1) * 4 + 2 + (ITERS - 1) * half * (2 * (n_blk - 1) + 1) + half + n_band * n_sub - 1
    )
    vmem = pl.BlockSpec(memory_space=pltpu.VMEM)
    hbm = pl.BlockSpec(memory_space=pltpu.HBM)
    out, new_temp = pl.pallas_call(
        functools.partial(kernel, (n_blk, n_band, n_sub, blocks, listed, size)),
        out_shape=(
            jax.ShapeDtypeStruct((bands, rows), jnp.float32),
            jax.ShapeDtypeStruct((1, rows), jnp.float32),
        ),
        in_specs=[hbm] * 11,
        out_specs=(vmem, vmem),
        scratch_shapes=[
            pltpu.VMEM(positions.shape, jnp.float32),
            pltpu.VMEM(angles.shape, jnp.float32),
            pltpu.VMEM(area.shape, jnp.float32),
            pltpu.SMEM(counts.shape, jnp.int32),
            pltpu.VMEM(direct.shape, jnp.float32),
            pltpu.VMEM(reflect.shape, jnp.float32),
            pltpu.SMEM(band_frac.shape, jnp.float32),
            pltpu.VMEM((1, rows), jnp.float32),
            pltpu.VMEM((1, rows), jnp.float32),
            pltpu.VMEM((total_blocks, 8, size), jnp.float32),
            pltpu.VMEM((3, rows), jnp.float32),
            pltpu.VMEM((8, 3 * size), jnp.float32),
            pltpu.VMEM((half, 64, 3 * size), jnp.bfloat16),
            pltpu.VMEM((half, slots * size, size), jnp.bfloat16),
            pltpu.VMEM((half, slots * size, size), jnp.bfloat16),
            pltpu.VMEM((n_sub, half, listed, size // 16, size), jnp.int32),
            pltpu.VMEM((n_sub, blocks, listed), jnp.int32),
            pltpu.SMEM((n_sub, blocks, listed), jnp.int32),
            pltpu.VMEM((blocks, bands, size), jnp.float32),
            pltpu.VMEM((n_band, n_sub, half, size), jnp.float32),
            pltpu.SemaphoreType.DMA((copies,)),
            pltpu.SemaphoreType.DMA((copies,)),
            pltpu.SemaphoreType.DMA((12,)),
        ]
        + [pltpu.VMEM((total_blocks, bands, size), jnp.float32)] * ITERS,
        compiler_params=pltpu.CompilerParams(
            collective_id=0, has_side_effects=True, vmem_limit_bytes=60 * 1024 * 1024
        ),
    )(positions, angles, area, vis_list, counts, occl, direct, reflect, band_frac, temp[None, :], heat[None, :])
    out, new_temp = pl.pallas_call(
        finish,
        out_shape=(
            jax.ShapeDtypeStruct((bands, rows), jnp.float32),
            jax.ShapeDtypeStruct((1, rows), jnp.float32),
        ),
        in_specs=[vmem, vmem],
        out_specs=(vmem, vmem),
    )(out, new_temp)
    return out[:band_count], new_temp.reshape(rows)


def solution(mesh):
    placed = (
        P(None, ("city", "blk")),
        P(None, ("city", "blk")),
        P(None, ("city", "blk")),
        P(("city", "blk"), "sub"),
        P(("city", "blk")),
        P(("city", "blk"), "sub", None, None),
        P("band", ("city", "blk")),
        P("band", ("city", "blk")),
        P("band"),
        P(("city", "blk")),
        P(("city", "blk")),
    )
    axes = (mesh.shape["blk"], mesh.shape["band"], mesh.shape["sub"])
    return jax.shard_map(
        functools.partial(local, axes),
        mesh=mesh,
        in_specs=placed,
        out_specs=(P("band", ("city", "blk")), P(("city", "blk"))),
        check_vma=False,
    )
```
